256 devices in a mesh: row: 16 (over x_lo, y, core), col: 16 (over z, x_hi).
Axes of the slice: x: 4 (x_hi: 2, x_lo: 2; x = x_hi * 2 + x_lo), y: 4, z: 8, core: 2. Of those that a mesh axis runs over, the one named last changes fastest.
Arguments:
- node_feats: bfloat16 [65536, 512], P(('row', 'col')), may hold values from -6 to 6
- cotangent: bfloat16 [65536, 512], P(('row', 'col')), may hold values from -6 to 6
- edge_base: bfloat16 [512, 512], replicated, may hold values from -0.25 to 0.25
- edge_down: bfloat16 [512, 16], replicated, may hold values from -0.25 to 0.25
- edge_up: bfloat16 [16, 512], replicated, may hold values from -1.5 to 1.5
- node_base: bfloat16 [1024, 512], replicated, may hold values from -0.1875 to 0.1875
- node_down: bfloat16 [1024, 16], replicated, may hold values from -0.1875 to 0.1875
- node_up: bfloat16 [16, 512], replicated, may hold values from -1.5 to 1.5
- tile_weight: bfloat16 [16, 16, 64, 128, 128], P('row', 'col'), may hold values from 0 to 1, as said below
- tile_place: int32 [16, 16, 64, 2], P('row', 'col'), may hold values from 0 to 31, as said below
- tile_count: int32 [16, 16], P('row', 'col'), may hold values from 1 to 64, as said below
Outputs:
- new_feats: bfloat16 [65536, 512], P(('row', 'col'))
- feat_grad: bfloat16 [65536, 512], P(('row', 'col'))
- edge_down_grad: float32 [512, 16], replicated
- edge_up_grad: float32 [16, 512], replicated
- node_down_grad: float32 [1024, 16], replicated
- node_up_grad: float32 [16, 512], replicated
The draws below stay inside these ranges and needn't reach their ends.
Inputs may be any that keep to these rules, and one draw needn't show every extreme that they name: `tile_place`: on each device the slots below its tile_count name distinct tiles; entry 0 is a tile row below 32, entry 1 a tile column below 32. `tile_count`: some device has all 64 slots live in every draw. `tile_weight`: Nonnegative; slots at or beyond a device's tile_count hold values that are no part of the graph.
All inputs are finite; a program needn't handle non-finite values.
Results may differ from the reference program's by a relative error of at most 0.035.
Values may be sent and summed in bfloat16 or wider, within the bound.
No kernel may reach another device: no remote copies, remote signals or barrier semaphores. Data moves between devices by JAX's collectives and lax.ppermute only.
A program may use at most 128 MiB of HBM per device.

```python
import math
import jax
import jax.numpy as jnp
from jax import lax

D = 512
RANK = 16
NODE_DEV = 256
TILE = 128
ROW_TILES = 32
COL_TILES = 32
SLOTS = 64
NODES = 65536
N_ROW = 16
N_COL = 16


def draw_cotangent(key, part):
    key = jax.random.fold_in(key, 11)
    key_base = jax.random.fold_in(key, 0)
    values = jax.random.normal(key_base, (NODES, D), jnp.float32)
    position = jnp.arange(NODES, dtype=jnp.float32) / NODES
    rising = jnp.exp(math.log(3.0) * position)[:, None]
    return jnp.clip(0.7 * values * rising, -6.0, 6.0).astype(jnp.bfloat16)


def draw_tile_weight(key, part):
    key = jax.random.fold_in(key, 5)
    key_mask, key_size = jax.random.split(key, 2)
    tile_shape = (N_ROW, N_COL, SLOTS, TILE, TILE)
    present = (jax.random.randint(key_mask, tile_shape, 0, 64) == 0).astype(jnp.float32)
    magnitude = jnp.exp(jax.random.uniform(key_size, tile_shape, jnp.float32, math.log(0.05), 0.0))
    return (present * magnitude).astype(jnp.bfloat16)


def draw_tile_place(key, part):
    key = jax.random.fold_in(key, 3)
    device_keys = jax.random.split(key, N_ROW * N_COL)
    flat_index = jnp.arange(ROW_TILES * COL_TILES, dtype=jnp.int32)
    tile_rows = flat_index // COL_TILES
    tile_cols = flat_index % COL_TILES
    distance = jnp.abs(tile_rows * COL_TILES // ROW_TILES - tile_cols)

    def one_device(device_key):
        noise = jax.random.randint(device_key, (ROW_TILES * COL_TILES,), 0, 2 * COL_TILES)
        scores = (noise + 4 * distance) * (ROW_TILES * COL_TILES) + flat_index
        chosen = jnp.argsort(scores, stable=True)[:SLOTS]
        return jnp.stack([chosen // COL_TILES, chosen % COL_TILES], axis=-1)
    places = jax.vmap(one_device)(device_keys)
    return places.reshape(N_ROW, N_COL, SLOTS, 2).astype(jnp.int32)


def draw_tile_count(key, part):
    key = jax.random.fold_in(key, 7)
    key_counts, key_busy = jax.random.split(key)
    lowest = max(1, SLOTS // 4)
    counts = jax.random.randint(key_counts, (N_ROW * N_COL,), lowest, SLOTS + 1)
    busiest = jax.random.randint(key_busy, (), 0, N_ROW * N_COL)
    counts = jnp.where(jnp.arange(N_ROW * N_COL) == busiest, SLOTS, counts)
    return counts.reshape(N_ROW, N_COL).astype(jnp.int32)


def steps_of(key, shape, shards, least, top_value):
    factor_of, own = 1.0, jax.random.fold_in(key, 6)
    for dim, parts in shards:
        heights = jnp.exp(jax.random.uniform(jax.random.fold_in(own, dim), (parts,), jnp.float32, least / len(shards), top_value / len(shards)))
        factor_of = factor_of * jnp.repeat(heights, shape[dim] // parts).reshape([-1 if axis == dim else 1 for axis in range(len(shape))])
    return factor_of


def centred(own_key, dims, scale, bound, cuts=(), kind=jnp.bfloat16):
    loudness = steps_of(own_key, dims, cuts, -0.22, 0.18) if cuts else 1.0
    entries = jax.random.normal(own_key, dims, jnp.float32) * scale * loudness
    return jnp.minimum(jnp.maximum(entries, -bound), bound).astype(kind)


def setup_inputs(seed: int = 0) -> dict:
    key_list = jax.random.split(jax.random.key(seed), 12)
    node_feats = centred(key_list[0], (NODES, D), 1.0, 6.0, ((0, 256),))
    cotangent = draw_cotangent(jax.random.fold_in(key_list[11], 71), 0)
    edge_base = centred(key_list[2], (D, D), D ** -0.5, 0.25)
    edge_down = centred(key_list[3], (D, RANK), D ** -0.5, 0.25)
    edge_up = centred(key_list[4], (RANK, D), RANK ** -0.5, 1.5)
    node_base = centred(key_list[5], (2 * D, D), (2 * D) ** -0.5, 0.1875)
    node_down = centred(key_list[6], (2 * D, RANK), (2 * D) ** -0.5, 0.1875)
    node_up = centred(key_list[7], (RANK, D), RANK ** -0.5, 1.5)
    tile_weight = draw_tile_weight(jax.random.fold_in(key_list[11], 71), 0)
    tile_place = draw_tile_place(jax.random.fold_in(key_list[11], 71), 0)
    tile_count = draw_tile_count(jax.random.fold_in(key_list[11], 71), 0)
    return {"node_feats": node_feats, "cotangent": cotangent, "edge_base": edge_base, "edge_down": edge_down, "edge_up": edge_up, "node_base": node_base, "node_down": node_down, "node_up": node_up, "tile_weight": tile_weight, "tile_place": tile_place, "tile_count": tile_count}


def silu_slope(values):
    sigma = jax.nn.sigmoid(values)
    return sigma * (1.0 + values * (1.0 - sigma))


def across(left, right):
    return lax.dot_general(left, right, (((0,), (0,)), ((), ())), preferred_element_type=jnp.float32)


def times_transposed(left, right):
    return lax.dot_general(left, right, (((1,), (1,)), ((), ())), preferred_element_type=jnp.float32)


def forward_sum(message, tile_weight, tile_place, tile_count):
    grid = message.reshape(N_ROW, N_COL, NODE_DEV, D)
    flat_tiles = tile_weight.reshape(N_ROW * N_COL, SLOTS, TILE, TILE)
    flat_place = tile_place.reshape(N_ROW * N_COL, SLOTS, 2)
    flat_count = tile_count.reshape(N_ROW * N_COL)
    device_ids = jnp.arange(N_ROW * N_COL, dtype=jnp.int32)

    def one_device(running, inputs):
        device_id, weights_all, places, count_here = inputs
        row_id = (device_id // N_COL).astype(jnp.int32)
        col_id = (device_id % N_COL).astype(jnp.int32)
        column_block = lax.dynamic_index_in_dim(grid, col_id, axis=1, keepdims=False)
        column_tiles = column_block.reshape(COL_TILES, TILE, D).astype(jnp.float32)
        alive_mask = jnp.arange(SLOTS, dtype=jnp.int32) < count_here
        weights_live = jnp.where(alive_mask[:, None, None], weights_all, jnp.zeros_like(weights_all)).astype(jnp.float32)
        fetched = column_tiles[places[:, 1]]
        products = jnp.einsum("gij,gjd->gid", weights_live, fetched)
        partial_value = jnp.zeros((ROW_TILES, TILE, D), jnp.float32).at[places[:, 0]].add(products)
        rounded = lax.optimization_barrier(partial_value.astype(jnp.bfloat16)).astype(jnp.float32)
        rounded = rounded.reshape(1, N_COL * NODE_DEV, D)
        current = lax.dynamic_slice_in_dim(running, row_id, 1, 0)
        running = lax.dynamic_update_slice_in_dim(running, current + rounded, row_id, 0)
        return running, None

    running = jnp.zeros((N_ROW, N_COL * NODE_DEV, D), jnp.float32)
    running = lax.scan(one_device, running, (device_ids, flat_tiles, flat_place, flat_count))[0]
    return running.reshape(NODES, D)


def backward_sum(agg_grad, tile_weight, tile_place, tile_count):
    rows_grid = agg_grad.reshape(N_ROW, N_COL * NODE_DEV, D)
    flat_tiles = tile_weight.reshape(N_ROW * N_COL, SLOTS, TILE, TILE)
    flat_place = tile_place.reshape(N_ROW * N_COL, SLOTS, 2)
    flat_count = tile_count.reshape(N_ROW * N_COL)
    device_ids = jnp.arange(N_ROW * N_COL, dtype=jnp.int32)

    def one_device(running, inputs):
        device_id, weights_all, places, count_here = inputs
        row_id = (device_id // N_COL).astype(jnp.int32)
        col_id = (device_id % N_COL).astype(jnp.int32)
        row_block = lax.dynamic_index_in_dim(rows_grid, row_id, axis=0, keepdims=False)
        row_tiles = row_block.reshape(ROW_TILES, TILE, D).astype(jnp.float32)
        alive_mask = jnp.arange(SLOTS, dtype=jnp.int32) < count_here
        weights_live = jnp.where(alive_mask[:, None, None], weights_all, jnp.zeros_like(weights_all)).astype(jnp.float32)
        fetched = row_tiles[places[:, 0]]
        products = jnp.einsum("gij,gid->gjd", weights_live, fetched)
        partial_value = jnp.zeros((COL_TILES, TILE, D), jnp.float32).at[places[:, 1]].add(products)
        rounded = lax.optimization_barrier(partial_value.astype(jnp.bfloat16)).astype(jnp.float32)
        rounded = rounded.reshape(N_ROW, 1, NODE_DEV, D)
        current = lax.dynamic_slice_in_dim(running, col_id, 1, 1)
        running = lax.dynamic_update_slice_in_dim(running, current + rounded, col_id, 1)
        return running, None

    running = jnp.zeros((N_ROW, N_COL, NODE_DEV, D), jnp.float32)
    running = lax.scan(one_device, running, (device_ids, flat_tiles, flat_place, flat_count))[0]
    return running.reshape(NODES, D)


def reference(node_feats, cotangent, edge_base, edge_down, edge_up, node_base, node_down, node_up, tile_weight, tile_place, tile_count):
    low_edge = jnp.dot(node_feats, edge_down, preferred_element_type=jnp.float32).astype(jnp.bfloat16)
    edge_pre = jnp.dot(node_feats, edge_base, preferred_element_type=jnp.float32) + jnp.dot(low_edge, edge_up, preferred_element_type=jnp.float32)
    message = jax.nn.silu(edge_pre).astype(jnp.bfloat16)
    aggregate = forward_sum(message, tile_weight, tile_place, tile_count)
    agg_round = aggregate.astype(jnp.bfloat16)
    joined = jnp.concatenate([node_feats, agg_round], axis=1)
    low_node = jnp.dot(joined, node_down, preferred_element_type=jnp.float32).astype(jnp.bfloat16)
    node_pre = jnp.dot(joined, node_base, preferred_element_type=jnp.float32) + jnp.dot(low_node, node_up, preferred_element_type=jnp.float32)
    new_feats = (node_feats.astype(jnp.float32) + jax.nn.silu(node_pre)).astype(jnp.bfloat16)
    node_slope = (cotangent.astype(jnp.float32) * silu_slope(node_pre)).astype(jnp.bfloat16)
    node_mix = times_transposed(node_slope, node_up).astype(jnp.bfloat16)
    joined_grad = times_transposed(node_slope, node_base) + times_transposed(node_mix, node_down)
    agg_grad = joined_grad[:, D:].astype(jnp.bfloat16)
    message_grad = backward_sum(agg_grad, tile_weight, tile_place, tile_count)
    edge_slope = (message_grad * silu_slope(edge_pre)).astype(jnp.bfloat16)
    edge_mix = times_transposed(edge_slope, edge_up).astype(jnp.bfloat16)
    factor = NODES ** -0.5
    edge_down_grad = across(node_feats, edge_mix) * factor
    edge_up_grad = across(low_edge, edge_slope) * factor
    node_down_grad = across(joined, node_mix) * factor
    node_up_grad = across(low_node, node_slope) * factor
    feat_grad = (cotangent.astype(jnp.float32) + joined_grad[:, :D] + times_transposed(edge_slope, edge_base) + times_transposed(edge_mix, edge_down)).astype(jnp.bfloat16)
    return (new_feats, feat_grad, edge_down_grad, edge_up_grad, node_down_grad, node_up_grad)
```

```python
import math

import jax
import jax.numpy as jnp
from jax import lax
from jax.experimental import pallas as pl
from jax.experimental.pallas import tpu as pltpu
from jax.sharding import Mesh, PartitionSpec as P

BF, F32 = jnp.bfloat16, jnp.float32
UNROLL = 8
MIB = 1 << 20
ALL = ("xly", "co", "zh", "zl", "xh")
ROW, COL = ("xly", "co"), ("zh", "zl", "xh")
ROW_GROUP = ("xly", "co", "zl")
COL_GROUP = ("co", "zh", "zl", "xh")


def dot(left, right):
    return jnp.dot(left, right, preferred_element_type=F32)


def across(left, right):
    return lax.dot_general(left, right, (((0,), (0,)), ((), ())), preferred_element_type=F32)


def times_transposed(left, right):
    return lax.dot_general(left, right, (((1,), (1,)), ((), ())), preferred_element_type=F32)


def sigmoid(values):
    return 1.0 / (1.0 + jnp.exp(-values))


def silu_slope(values):
    sigma = sigmoid(values)
    return sigma * (1.0 + values * (1.0 - sigma))


def call(kernel, out_shape, *args, scratch=(), smem=0, vmem=40, flops=0, name=None):
    moved = sum(a.size * a.dtype.itemsize for a in args)
    moved += sum(math.prod(s.shape) * s.dtype.itemsize for s in jax.tree.leaves(out_shape))
    return pl.pallas_call(
        kernel,
        out_shape=out_shape,
        in_specs=[pl.BlockSpec(memory_space=pltpu.SMEM)] * smem
        + [pl.BlockSpec(memory_space=pltpu.VMEM)] * (len(args) - smem),
        out_specs=jax.tree.map(lambda _: pl.BlockSpec(memory_space=pltpu.VMEM), out_shape),
        scratch_shapes=list(scratch),
        compiler_params=pltpu.CompilerParams(vmem_limit_bytes=vmem * MIB),
        cost_estimate=pl.CostEstimate(flops=flops, bytes_accessed=moved, transcendentals=0),
        name=name,
    )(*args)


def message_kernel(feats, base, down, up, pieces, pre_out, low_out):
    low = dot(feats[...], down[...]).astype(BF)
    pre = dot(feats[...], base[...]) + dot(low, up[...])
    message = (pre * sigmoid(pre)).astype(BF)
    low_out[...] = low
    pre_out[...] = pre
    quarters, width = 4, pieces.shape[-1]
    for i in range(pieces.shape[0]):
        q = i % quarters
        pieces[i] = message[:, q * width : (q + 1) * width]


def tile_kernel(backward, here, meta, w0, w1, w2, w3, source, out, total):
    co, zl = here[0], here[1]
    rows = out.shape[0]
    block_rows = rows // 2
    chunk = 512
    slots = w0.shape[0]

    def clear(i, carry):
        total[pl.ds(pl.multiple_of(i * chunk, chunk), chunk), :] = jnp.zeros(
            (chunk, total.shape[1]), F32
        )
        return carry

    lax.fori_loop(0, rows // chunk, clear, 0)

    for weights, other_co, other_zl in ((w0, 0, 0), (w1, 1, 0), (w2, 0, 1), (w3, 1, 1)):
        owner_co = co ^ other_co
        owner_zl = zl ^ other_zl
        owner = owner_co * 2 + owner_zl
        count = meta[owner, 2 * slots]

        def group(i, carry, weights=weights, owner=owner, owner_co=owner_co, owner_zl=owner_zl, count=count):
            products, places = [], []
            for j in range(UNROLL):
                slot = i * UNROLL + j
                live = slot < count
                tile_row = jnp.where(live, meta[owner, 2 * slot], 0)
                tile_col = jnp.where(live, meta[owner, 2 * slot + 1], 0)
                row_at = owner_co * block_rows + tile_row * 128
                col_at = (tile_col >> 1) * 512 + owner_zl * 256 + (tile_col & 1) * 128
                from_at, to_at = (row_at, col_at) if backward else (col_at, row_at)
                places.append(pl.multiple_of(jnp.where(live, to_at, rows), 128))
                block = source[pl.ds(pl.multiple_of(from_at, 128), 128), :]
                tile = weights[slot]
                products.append(across(tile, block) if backward else dot(tile, block))
            for product, at in zip(products, places):
                total[pl.ds(at, 128), :] += product
            return carry

        lax.fori_loop(0, (count + UNROLL - 1) // UNROLL, group, 0)

    def finish(i, carry):
        at = pl.ds(pl.multiple_of(i * chunk, chunk), chunk)
        out[at, :] = total[at, :].astype(BF)
        return carry

    lax.fori_loop(0, rows // chunk, finish, 0)


def node_kernel(feats, cot, parts, base, down, up, new_out, pieces, partial_out, grads):
    n_col = parts.shape[0] // 2
    width = parts.shape[-1]
    quarters = []
    for s_co in range(2):
        for s_zl in range(2):
            value = None
            for zh in range(n_col // 4):
                for xh in range(2):
                    term = parts[s_co * n_col + zh * 4 + s_zl * 2 + xh].astype(F32)
                    value = term if value is None else value + term
            quarters.append(value.astype(BF))
    joined = jnp.concatenate([feats[...]] + quarters, axis=1)
    low = dot(joined, down[...]).astype(BF)
    pre = dot(joined, base[...]) + dot(low, up[...])
    sigma = sigmoid(pre)
    new_out[...] = (feats[...].astype(F32) + pre * sigma).astype(BF)
    cot_wide = cot[...].astype(F32)
    slope = (cot_wide * (sigma * (1.0 + pre * (1.0 - sigma)))).astype(BF)
    mix = times_transposed(slope, up[...]).astype(BF)
    joined_grad = times_transposed(slope, base[...]) + times_transposed(mix, down[...])
    full = feats.shape[1]
    partial_out[...] = cot_wide + joined_grad[:, :full]
    agg_grad = joined_grad[:, full:].astype(BF)
    for i in range(pieces.shape[0]):
        q = (i // n_col) * 2 + (i >> 1) % 2
        pieces[i] = agg_grad[:, q * width : (q + 1) * width]
    grads[:, : 2 * full] = across(mix, joined)
    grads[:, 2 * full :] = across(low, slope)


def edge_kernel(feats, parts, pre, low, partial, base, down, up, feat_out, grads):
    width = parts.shape[-1]
    quarters = []
    for q in range(4):
        value = None
        for i in range(parts.shape[0] // 4):
            term = parts[i * 4 + q].astype(F32)
            value = term if value is None else value + term
        quarters.append(value)
    slopes = []
    for q in range(4):
        slopes.append((quarters[q] * silu_slope(pre[:, q * width : (q + 1) * width])).astype(BF))
    slope = jnp.concatenate(slopes, axis=1)
    mix = times_transposed(slope, up[...]).astype(BF)
    full = feats.shape[1]
    grads[:, :full] = across(mix, feats[...])
    grads[:, full:] = across(low[...], slope)
    feat_out[...] = (
        partial[...] + times_transposed(slope, base[...]) + times_transposed(mix, down[...])
    ).astype(BF)


def exchange(pieces, axes):
    shape = pieces.shape
    flat = pieces.reshape(shape[0] * shape[1], shape[2])
    return lax.all_to_all(flat, axes, split_axis=0, concat_axis=0, tiled=True)


def sum_over_all(grads, n_row, n_col):
    rank, wide = grads.shape
    lines = -(-wide // 1024) * 8
    part = rank // n_row * lines
    grads = jnp.pad(grads, ((0, 0), (0, lines * 128 - wide)))
    mine = exchange(grads.reshape(n_row, part, 128), ROW)
    mine = mine.reshape(n_row, part, 128).sum(axis=0)
    spread = jnp.broadcast_to(mine[None], (n_col, part, 128))
    mine = exchange(spread, COL).reshape(n_col, part, 128).sum(axis=0)
    spread = jnp.broadcast_to(mine[None], (n_row, part, 128))
    whole = exchange(spread, ROW).reshape(rank, lines * 128)
    return whole[:, :wide]


def body(
    node_feats,
    cotangent,
    edge_base,
    edge_down,
    edge_up,
    node_base,
    node_down,
    node_up,
    tile_weight,
    tile_place,
    tile_count,
):
    nodes, full = node_feats.shape
    n_row = lax.axis_size(ROW)
    n_col = lax.axis_size(COL)
    rank = edge_up.shape[0]
    width = full // 4
    tiles = tile_weight[0, 0]
    slots = tiles.shape[0]
    sds = jax.ShapeDtypeStruct

    def swap(values, axis):
        return lax.ppermute(values, axis, [(0, 1), (1, 0)])

    tiles_z = swap(tiles, "zl")
    tiles_c = swap(tiles, "co")
    tiles_cz = swap(tiles_z, "co")
    meta = jnp.concatenate([tile_place.reshape(1, 2 * slots), tile_count.reshape(1, 1)], axis=1)
    meta = jnp.pad(meta, ((0, 0), (0, 256 - meta.shape[1])))
    meta = lax.all_gather(meta, ("co", "zl"), axis=0, tiled=True)
    here = jnp.stack([lax.axis_index("co"), lax.axis_index("zl")]).astype(jnp.int32)

    pieces, pre, low = call(
        message_kernel,
        (
            sds((2 * n_row, nodes, width), BF),
            sds((nodes, full), F32),
            sds((nodes, rank), BF),
        ),
        node_feats,
        edge_base,
        edge_down,
        edge_up,
        name="message",
    )
    source = exchange(pieces, ROW_GROUP)

    def tile_sum(backward, values, rows):
        def kernel(*refs):
            tile_kernel(backward, *refs)

        return call(
            kernel,
            sds((rows, width), BF),
            here,
            meta,
            tiles,
            tiles_c,
            tiles_z,
            tiles_cz,
            values,
            scratch=[pltpu.VMEM((rows + 128, width), F32)],
            smem=2,
            flops=2 * 4 * slots * 128 * 128 * width,
            name="tiles_back" if backward else "tiles",
        )

    partial_rows = tile_sum(False, source, 2 * n_col * nodes)
    parts = lax.all_to_all(partial_rows, COL_GROUP, split_axis=0, concat_axis=0, tiled=True)
    new_feats, pieces, partial_grad, node_grads = call(
        node_kernel,
        (
            sds((nodes, full), BF),
            sds((2 * n_col, nodes, width), BF),
            sds((nodes, full), F32),
            sds((rank, 3 * full), F32),
        ),
        node_feats,
        cotangent,
        parts.reshape(2 * n_col, nodes, width),
        node_base,
        node_down,
        node_up,
        name="node",
    )
    source = exchange(pieces, COL_GROUP)
    partial_cols = tile_sum(True, source, 2 * n_row * nodes)
    parts = lax.all_to_all(partial_cols, ROW_GROUP, split_axis=0, concat_axis=0, tiled=True)
    feat_grad, edge_grads = call(
        edge_kernel,
        (sds((nodes, full), BF), sds((rank, 2 * full), F32)),
        node_feats,
        parts.reshape(2 * n_row, nodes, width),
        pre,
        low,
        partial_grad,
        edge_base,
        edge_down,
        edge_up,
        name="edge",
    )
    grads = sum_over_all(jnp.concatenate([edge_grads, node_grads], axis=1), n_row, n_col)
    grads = grads * (1.0 / math.sqrt(nodes * n_row * n_col))
    return (
        new_feats,
        feat_grad,
        grads[:, :full].T,
        grads[:, full : 2 * full],
        grads[:, 2 * full : 4 * full].T,
        grads[:, 4 * full :],
    )


def solution(mesh):
    n_row, n_col = mesh.shape["row"], mesh.shape["col"]
    fine = Mesh(mesh.devices.reshape(n_row // 2, 2, n_col // 4, 2, 2), ALL)
    nodes = P(ROW + COL, None)
    placed = (
        nodes,
        nodes,
        P(),
        P(),
        P(),
        P(),
        P(),
        P(),
        P(ROW, COL, None, None, None),
        P(ROW, COL, None, None),
        P(ROW, COL),
    )
    return jax.shard_map(
        body,
        mesh=fine,
        in_specs=placed,
        out_specs=(nodes, nodes, P(), P(), P(), P()),
        check_vma=False,
    )
```

```python
import math

import jax
import jax.numpy as jnp
from jax import lax
from jax.experimental import pallas as pl
from jax.experimental.pallas import tpu as pltpu
from jax.sharding import Mesh, PartitionSpec as P

BF, F32 = jnp.bfloat16, jnp.float32
UNROLL = 8
PARTS = 4
MIB = 1 << 20
ALL = ("xly", "co", "z", "xh")
ROW, COL = ("xly", "co"), ("z", "xh")


def dot(left, right):
    return jnp.dot(left, right, preferred_element_type=F32)


def across(left, right):
    return lax.dot_general(left, right, (((0,), (0,)), ((), ())), preferred_element_type=F32)


def times_transposed(left, right):
    return lax.dot_general(left, right, (((1,), (1,)), ((), ())), preferred_element_type=F32)


def sigmoid(values):
    return 1.0 / (1.0 + jnp.exp(-values))


def silu_slope(values):
    sigma = sigmoid(values)
    return sigma * (1.0 + values * (1.0 - sigma))


def call(kernel, out_shape, *args, scratch=(), smem=0, vmem=40, flops=0, name=None, far=()):
    def place(i):
        return pl.BlockSpec(memory_space=pltpu.HBM if i in far else pltpu.VMEM)

    moved = sum(a.size * a.dtype.itemsize for a in args)
    moved += sum(math.prod(s.shape) * s.dtype.itemsize for s in jax.tree.leaves(out_shape))
    return pl.pallas_call(
        kernel,
        out_shape=out_shape,
        in_specs=[pl.BlockSpec(memory_space=pltpu.SMEM)] * smem
        + [place(i) for i in range(smem, len(args))],
        out_specs=(pl.BlockSpec(memory_space=pltpu.VMEM),) * len(out_shape),
        scratch_shapes=list(scratch),
        compiler_params=pltpu.CompilerParams(vmem_limit_bytes=vmem * MIB),
        cost_estimate=pl.CostEstimate(flops=flops, bytes_accessed=moved, transcendentals=0),
        name=name,
    )(*args)


def add(*terms):
    total = terms[0].astype(F32)
    for term in terms[1:]:
        total = total + term.astype(F32)
    return total


def message_kernel(feats, base, down_t, up, pieces):
    low = times_transposed(feats[...], down_t[...]).astype(BF)
    pre = dot(feats[...], base[...]) + dot(low, up[...])
    message = (pre * sigmoid(pre)).astype(BF)
    width = pieces.shape[2]
    for i in range(pieces.shape[0]):
        pieces[i] = message[:, i % 2 * width : (i % 2 + 1) * width]


def clear(total):
    rows = total.shape[0] - 128

    def step(i, carry):
        at = pl.ds(pl.multiple_of(i * 256, 256), 256)
        total[at, :] = jnp.zeros((256, total.shape[1]), F32)
        return carry

    lax.fori_loop(0, rows // 256, step, 0)


def fetch_tiles(stacks, near, sems):
    size = near.shape[1] // PARTS
    copies = []
    for owner, stack in enumerate(stacks):
        for part in range(PARTS):
            at = pl.ds(part * size, size)
            copy = pltpu.make_async_copy(
                stack.at[at], near.at[owner, at], sems.at[owner * PARTS + part]
            )
            copy.start()
            copies.append(copy)
    return copies


def add_tiles(meta, owner, weights, copies, source, source_at, total, backward):
    slots = weights.shape[0]
    spare = total.shape[0] - 128
    count = meta[owner, 2 * slots]
    size = slots // PARTS

    def group(i, carry):
        products, places = [], []
        for j in range(UNROLL):
            slot = i * UNROLL + j
            live = slot < count
            tile_row = jnp.where(live, meta[owner, 2 * slot], 0)
            tile_col = jnp.where(live, meta[owner, 2 * slot + 1], 0)
            from_tile, to_tile = (tile_row, tile_col) if backward else (tile_col, tile_row)
            places.append(pl.multiple_of(jnp.where(live, to_tile * 128, spare), 128))
            block = source[pl.ds(pl.multiple_of(source_at + from_tile * 128, 128), 128), :]
            tile = weights[slot]
            products.append(across(tile, block) if backward else dot(tile, block))
        for product, at in zip(products, places):
            total[pl.ds(at, 128), :] += product
        return carry

    for part, copy in enumerate(copies):
        copy.wait()
        end = jnp.minimum(count, (part + 1) * size)
        lax.fori_loop(part * size // UNROLL, (end + UNROLL - 1) // UNROLL, group, 0)


def forward_kernel(owner, groups, n_z, here, meta, stack, source, *rest):
    outs, (total, near, sems) = rest[:-3], rest[-3:]
    copies = fetch_tiles([stack], near, sems)
    z, xh = here[1], here[2]
    nodes = (total.shape[0] - 128) // (2 * n_z)
    clear(total)
    add_tiles(meta, owner, near.at[0], copies, source, 0, total, False)
    for out, places in zip(outs, groups):
        for k, (distance, side) in enumerate(places):
            to = lax.rem(z + (distance + n_z), n_z) * 2 + (xh ^ side)
            block = total[pl.ds(pl.multiple_of(to * nodes, nodes), nodes), :]
            out[k * nodes : (k + 1) * nodes] = block.astype(BF)


def backward_kernel(places, n_z, here, meta, stack, stack_other, *rest):
    shards, (out, total, source, near, sems) = rest[:-5], rest[-5:]
    copies = fetch_tiles([stack, stack_other], near, sems)
    z, xh = here[1], here[2]
    nodes = source.shape[0] // (4 * n_z)
    for shard, wanted in zip(shards, places):
        for k, (owner, distance, side) in enumerate(wanted):
            at = (owner * n_z + lax.rem(z + (distance + n_z), n_z)) * 2 + (xh ^ side)
            source[pl.ds(pl.multiple_of(at * nodes, nodes), nodes), :] = shard[
                k * nodes : (k + 1) * nodes
            ]
    clear(total)
    add_tiles(meta, 0, near.at[0], copies[:PARTS], source, 0, total, True)
    add_tiles(meta, 1, near.at[1], copies[PARTS:], source, 2 * n_z * nodes, total, True)

    def finish(i, carry):
        at = pl.ds(pl.multiple_of(i * 256, 256), 256)
        out[at, :] = total[at, :].astype(BF)
        return carry

    lax.fori_loop(0, out.shape[0] // 256, finish, 0)


def node_kernel(here, feats, cot, t0, t1, t2, t3, other, base, down_t, up, new_out, keep, give, partial_out, grads):
    first = here[0] == 0
    full = feats.shape[1]
    half = full // 2
    nodes = feats.shape[0]
    mine = add(t0[:nodes], t1[:nodes], t2[:nodes], t3[...]).astype(BF)
    rest = other[...]
    agg = [jnp.where(first, mine, rest), jnp.where(first, rest, mine)]
    joined = jnp.concatenate([feats[...]] + agg, axis=1)
    low = times_transposed(joined, down_t[...]).astype(BF)
    pre = dot(joined, base[...]) + dot(low, up[...])
    sigma = sigmoid(pre)
    cot_wide = cot[...].astype(F32)
    slope = (cot_wide * (sigma * (1.0 + pre * (1.0 - sigma)))).astype(BF)
    mix = times_transposed(slope, up[...]).astype(BF)
    joined_grad = times_transposed(slope, base[...]) + dot(mix, down_t[...])
    agg_grad = joined_grad[:, full:].astype(BF)
    keep[...] = jnp.where(first, agg_grad[:, :half], agg_grad[:, half:])
    give[...] = jnp.where(first, agg_grad[:, half:], agg_grad[:, :half])
    new_out[...] = (feats[...].astype(F32) + pre * sigma).astype(BF)
    partial_out[...] = cot_wide + joined_grad[:, :full]
    grads[:, : 2 * full] = across(mix, joined)
    grads[:, 2 * full :] = across(low, slope)


def edge_kernel(feats, parts, partial, base, down_t, up, feat_out, grads):
    full = feats.shape[1]
    low = times_transposed(feats[...], down_t[...]).astype(BF)
    pre = dot(feats[...], base[...]) + dot(low, up[...])
    factor = silu_slope(pre)
    halves = [None] * 2
    for i in range(parts.shape[0]):
        term = parts[i].astype(F32)
        halves[i % 2] = term if halves[i % 2] is None else halves[i % 2] + term
    slope = (jnp.concatenate(halves, axis=1) * factor).astype(BF)
    mix = times_transposed(slope, up[...]).astype(BF)
    grads[:, :full] = across(mix, feats[...])
    grads[:, full:] = across(low, slope)
    feat_out[...] = (
        partial[...] + times_transposed(slope, base[...]) + dot(mix, down_t[...])
    ).astype(BF)


def exchange(pieces, axes):
    shape = pieces.shape
    flat = pieces.reshape(shape[0] * shape[1], shape[2])
    return lax.all_to_all(flat, axes, split_axis=0, concat_axis=0, tiled=True)


def sum_over_all(grads):
    near = ("xly", "co", "xh")
    n_near, n_z = lax.axis_size(near), lax.axis_size("z")
    rank, wide = grads.shape
    lines = -(-rank * wide // (n_near * 1024)) * 8
    grads = jnp.pad(grads.reshape(-1), (0, n_near * lines * 128 - rank * wide))
    mine = exchange(grads.reshape(n_near, lines, 128), near)
    mine = mine.reshape(n_near, lines, 128).sum(axis=0)
    spread = jnp.broadcast_to(mine[None], (n_z, lines, 128))
    mine = exchange(spread, "z").reshape(n_z, lines, 128).sum(axis=0)
    spread = jnp.broadcast_to(mine[None], (n_near, lines, 128))
    whole = exchange(spread, near).reshape(-1)
    return whole[: rank * wide].reshape(rank, wide)


def body(
    node_feats,
    cotangent,
    edge_base,
    edge_down,
    edge_up,
    node_base,
    node_down,
    node_up,
    tile_weight,
    tile_place,
    tile_count,
):
    nodes, full = node_feats.shape
    n_row = lax.axis_size(ROW)
    n_col = lax.axis_size(COL)
    n_z = lax.axis_size("z")
    n_up, n_down = n_z // 2, (n_z - 1) // 2
    rank = edge_up.shape[0]
    half = full // 2
    tiles = tile_weight[0, 0]
    slots = tiles.shape[0]
    sds = jax.ShapeDtypeStruct

    def swap(values, axis):
        return lax.ppermute(values, axis, [(0, 1), (1, 0)])

    def up(values):
        return lax.ppermute(values, "z", [(i, (i + 1) % n_z) for i in range(n_z)])

    def down(values):
        return lax.ppermute(values, "z", [((i + 1) % n_z, i) for i in range(n_z)])

    meta = jnp.concatenate([tile_place.reshape(1, 2 * slots), tile_count.reshape(1, 1)], axis=1)
    meta = jnp.pad(meta, ((0, 0), (0, 256 - meta.shape[1])))
    meta = jnp.concatenate([meta, swap(meta, "co")], axis=0)
    tiles_c = swap(tiles, "co")
    here = jnp.stack([lax.axis_index("co"), lax.axis_index("z"), lax.axis_index("xh")])
    here = here.astype(jnp.int32)

    pieces = call(
        message_kernel,
        (sds((n_row, nodes, half), BF),),
        node_feats,
        edge_base,
        edge_down.T,
        edge_up,
        name="message",
    )[0]
    source = exchange(pieces, ROW)

    def forward_sum(owner, weights, source, groups, name):
        rows = n_col * nodes

        def kernel(*refs):
            forward_kernel(owner, groups, n_z, *refs)

        return call(
            kernel,
            tuple(sds((len(places) * nodes, half), BF) for places in groups),
            here,
            meta,
            weights,
            source,
            scratch=[
                pltpu.VMEM((rows + 128, half), F32),
                pltpu.VMEM((1, slots, 128, 128), BF),
                pltpu.SemaphoreType.DMA((PARTS,)),
            ],
            smem=2,
            far=(2,),
            flops=2 * slots * 128 * 128 * half,
            name=name,
        )

    flat = [d for i in range(n_up) for d in (n_up - i, i - n_down)]
    pairs = [flat[: n_z // 2], flat[n_z // 2 :]]
    outs = forward_sum(
        1, tiles_c, source, [[(d, 1) for d in group] for group in pairs] + [[(d, 0)] for d in flat], "tiles_other"
    )
    kept = dict(zip(flat, outs[2:]))
    other = {}
    for group, sent in zip(pairs, outs[:2]):
        got = swap(sent, "xh")
        for k, d in enumerate(group):
            other[d] = add(kept[d], got[k * nodes : (k + 1) * nodes]).astype(BF)
    source = lax.optimization_barrier((source,) + tuple(outs[:2]))[0]
    outs = forward_sum(0, tiles, source, [[(d, 0), (d, 1)] for d in flat], "tiles_own")
    own = dict(zip(flat, outs))

    def ring_sum(blocks):
        rising = up(blocks[n_up])
        falling = down(blocks[-n_down]) if n_down else None
        for k in range(1, n_up):
            rising = up(add(rising, blocks[n_up - k]).astype(BF))
            if k < n_down:
                falling = down(add(falling, blocks[k - n_down]).astype(BF))
        return [blocks[0], rising] + ([falling] if n_down else [])

    other_terms = ring_sum(other)
    own_terms = ring_sum(own)
    agg_other = swap(add(*other_terms).astype(BF), "co")
    across_x = swap(add(*[term[nodes:] for term in own_terms]).astype(BF), "xh")
    if not n_down:
        own_terms = own_terms + [jnp.zeros_like(own_terms[0])]
    new_feats, keep, give, partial_grad, node_grads = call(
        node_kernel,
        (
            sds((nodes, full), BF),
            sds((nodes, half), BF),
            sds((nodes, half), BF),
            sds((nodes, full), F32),
            sds((rank, 3 * full), F32),
        ),
        here,
        node_feats,
        cotangent,
        *own_terms,
        across_x,
        agg_other,
        node_base,
        node_down.T,
        node_up,
        smem=1,
        name="node",
    )

    def ring_gather(block):
        blocks = {0: block}
        for k in range(1, n_up + 1):
            blocks[-k] = up(blocks[1 - k])
            if k <= n_down:
                blocks[k] = down(blocks[k - 1])
        return blocks

    own = ring_gather(jnp.concatenate([keep, swap(keep, "xh")], axis=0))
    other = ring_gather(swap(give, "co"))
    shards, places = [], []
    for d in own:
        shards.append(own[d])
        places.append([(0, d, 0), (0, d, 1)])
    groups = [[0, -1] if n_down < 1 else [0, 1, -1]] + [[k, -k] for k in range(2, n_down + 1)]
    if n_up > max(1, n_down):
        groups.append([-n_up])
    for group in groups:
        shards += [other[d] for d in group]
        places += [[(1, d, 0)] for d in group]
        shards.append(swap(jnp.concatenate([other[d] for d in group]), "xh"))
        places.append([(1, d, 1) for d in group])

    def backward(*refs):
        backward_kernel(places, n_z, *refs)

    rows = n_row * nodes
    partial_cols = call(
        backward,
        (sds((rows, half), BF),),
        here,
        meta,
        tiles,
        tiles_c,
        *shards,
        scratch=[
            pltpu.VMEM((rows + 128, half), F32),
            pltpu.VMEM((2 * n_col * nodes, half), BF),
            pltpu.VMEM((2, slots, 128, 128), BF),
            pltpu.SemaphoreType.DMA((2 * PARTS,)),
        ],
        smem=2,
        far=(2, 3),
        flops=4 * slots * 128 * 128 * half,
        name="tiles_back",
    )[0]
    parts = lax.all_to_all(partial_cols, ROW, split_axis=0, concat_axis=0, tiled=True)
    feat_grad, edge_grads = call(
        edge_kernel,
        (sds((nodes, full), BF), sds((rank, 2 * full), F32)),
        node_feats,
        parts.reshape(n_row, nodes, half),
        partial_grad,
        edge_base,
        edge_down.T,
        edge_up,
        name="edge",
    )
    grads = sum_over_all(jnp.concatenate([edge_grads, node_grads], axis=1))
    grads = grads * (1.0 / math.sqrt(nodes * n_row * n_col))
    return (
        new_feats,
        feat_grad,
        grads[:, :full].T,
        grads[:, full : 2 * full],
        grads[:, 2 * full : 4 * full].T,
        grads[:, 4 * full :],
    )


def solution(mesh):
    n_row, n_col = mesh.shape["row"], mesh.shape["col"]
    fine = Mesh(mesh.devices.reshape(n_row // 2, 2, n_col // 2, 2), ALL)
    nodes = P(ROW + COL, None)
    placed = (
        nodes,
        nodes,
        P(),
        P(),
        P(),
        P(),
        P(),
        P(),
        P(ROW, COL, None, None, None),
        P(ROW, COL, None, None),
        P(ROW, COL),
    )
    return jax.shard_map(
        body,
        mesh=fine,
        in_specs=placed,
        out_specs=(nodes, nodes, P(), P(), P(), P()),
        check_vma=False,
    )
```

```python
import math

import jax
import jax.numpy as jnp
from jax import lax
from jax.experimental import pallas as pl
from jax.experimental.pallas import tpu as pltpu
from jax.sharding import Mesh, PartitionSpec as P

BF, F32 = jnp.bfloat16, jnp.float32
UNROLL = 16
PARTS = 2
MIB = 1 << 20
ALL = ("xly", "co", "z", "xh")
ROW, COL = ("xly", "co"), ("z", "xh")
NEAR = ("xly", "co", "xh")
SHARED = ((0, 0), (1, 0), (0, 1), (1, 1))


def dot(left, right):
    return jnp.dot(left, right, preferred_element_type=F32)


def across(left, right):
    return lax.dot_general(left, right, (((0,), (0,)), ((), ())), preferred_element_type=F32)


def times_transposed(left, right):
    return lax.dot_general(left, right, (((1,), (1,)), ((), ())), preferred_element_type=F32)


def sigmoid(values):
    return 1.0 / (1.0 + jnp.exp(-values))


def silu_slope(values):
    sigma = sigmoid(values)
    return sigma * (1.0 + values * (1.0 - sigma))


def call(kernel, out_shape, *args, scratch=(), smem=0, vmem=40, flops=0, name=None, far=()):
    def place(i):
        return pl.BlockSpec(memory_space=pltpu.HBM if i in far else pltpu.VMEM)

    moved = sum(a.size * a.dtype.itemsize for a in args)
    moved += sum(math.prod(s.shape) * s.dtype.itemsize for s in jax.tree.leaves(out_shape))
    return pl.pallas_call(
        kernel,
        out_shape=out_shape,
        in_specs=[pl.BlockSpec(memory_space=pltpu.SMEM)] * smem
        + [place(i) for i in range(smem, len(args))],
        out_specs=(pl.BlockSpec(memory_space=pltpu.VMEM),) * len(out_shape),
        scratch_shapes=list(scratch),
        compiler_params=pltpu.CompilerParams(vmem_limit_bytes=vmem * MIB),
        cost_estimate=pl.CostEstimate(flops=flops, bytes_accessed=moved, transcendentals=0),
        name=name,
    )(*args)


def add(*terms):
    total = terms[0].astype(F32)
    for term in terms[1:]:
        total = total + term.astype(F32)
    return total


def message_kernel(feats, base, down_t, up, pieces):
    low = times_transposed(feats[...], down_t[...]).astype(BF)
    pre = dot(feats[...], base[...]) + dot(low, up[...])
    message = (pre * sigmoid(pre)).astype(BF)
    width = pieces.shape[2]
    for i in range(pieces.shape[0]):
        pieces[i] = message[:, i % 2 * width : (i % 2 + 1) * width]


def clear(total):
    rows = total.shape[0] - 128

    def step(i, carry):
        at = pl.ds(pl.multiple_of(i * 256, 256), 256)
        total[at, :] = jnp.zeros((256, total.shape[1]), F32)
        return carry

    lax.fori_loop(0, rows // 256, step, 0)


def fetch_tiles(meta, stacks, near, sems):
    slots = near.shape[1]
    size = slots // PARTS
    copies = []
    for owner, stack in enumerate(stacks):
        for part in range(PARTS):
            at = pl.ds(part * size, size)
            source = stack[0].at[at] if len(stack) == 1 else stack[part]
            live = meta[owner, 2 * slots] > part * size
            copy = pltpu.make_async_copy(
                source, near.at[owner, at], sems.at[owner * PARTS + part]
            )
            pl.when(live)(copy.start)
            copies.append((live, copy))
    return copies


def add_tiles(meta, owner, weights, copies, source, total, row_at, col_at, backward):
    slots = weights.shape[0]
    spare = total.shape[0] - 128
    count = meta[owner, 2 * slots]
    size = slots // PARTS

    def group(i, carry):
        products, places = [], []
        for j in range(UNROLL):
            slot = i * UNROLL + j
            live = slot < count
            row = row_at(jnp.where(live, meta[owner, 2 * slot], 0))
            col = col_at(jnp.where(live, meta[owner, 2 * slot + 1], 0))
            begin, end = (row, col) if backward else (col, row)
            places.append(pl.multiple_of(jnp.where(live, end, spare), 128))
            block = source[pl.ds(pl.multiple_of(begin, 128), 128), :]
            tile = weights[slot]
            products.append(across(tile, block) if backward else dot(tile, block))
        for product, at in zip(products, places):
            total[pl.ds(at, 128), :] += product
        return carry

    for part, (wanted, copy) in enumerate(copies):
        pl.when(wanted)(copy.wait)
        end = jnp.minimum(count, (part + 1) * size)
        lax.fori_loop(part * size // UNROLL, (end + UNROLL - 1) // UNROLL, group, 0)


def forward_kernel(groups, n_z, here, meta, w0, w1, source, *rest):
    outs, (total, near, sems) = rest[:-3], rest[-3:]
    copies = fetch_tiles(meta, [[w0], [w1]], near, sems)
    z, xh = here[1], here[2]
    nodes = (total.shape[0] - 128) // (4 * n_z)
    clear(total)
    for owner in range(2):

        def row_at(tile, owner=owner):
            return owner * (2 * n_z * nodes) + tile * 128

        def col_at(tile):
            return tile * 128

        parts = copies[owner * PARTS : (owner + 1) * PARTS]
        add_tiles(meta, owner, near.at[owner], parts, source, total, row_at, col_at, False)
    for out, places in zip(outs, groups):
        for k, (owner, distance, side) in enumerate(places):
            to = lax.rem(z + (distance + n_z), n_z) * 2 + (xh ^ side)
            at = pl.multiple_of((owner * 2 * n_z + to) * nodes, nodes)
            out[k * nodes : (k + 1) * nodes] = total[pl.ds(at, nodes), :].astype(BF)


def backward_kernel(distances, n_z, here, meta, w0, w1, w2, w3, w4, w5, *rest):
    shards, (out, total, source, near, sems) = rest[:-5], rest[-5:]
    copies = fetch_tiles(meta, [[w0], [w1], [w2, w3], [w4, w5]], near, sems)
    z, xh = here[1], here[2]
    block = source.shape[0] // n_z
    nodes = block // 4
    for shard, distance in zip(shards, distances):
        at = lax.rem(z + (distance + n_z), n_z) * block
        source[pl.ds(pl.multiple_of(at, block), block), :] = shard[...]
    clear(total)
    for owner, (core, side) in enumerate(SHARED):

        def row_at(tile, core=core):
            place = core * 2 + (((tile >> 1) & 1) ^ xh)
            return (tile >> 2) * block + place * nodes + (tile & 1) * 128

        def col_at(tile, side=side):
            return ((tile >> 1) * 2 + (xh ^ side)) * nodes + (tile & 1) * 128

        parts = copies[owner * PARTS : (owner + 1) * PARTS]
        add_tiles(meta, owner, near.at[owner], parts, source, total, row_at, col_at, True)

    def finish(i, carry):
        at = pl.ds(pl.multiple_of(i * 256, 256), 256)
        out[at, :] = total[at, :].astype(BF)
        return carry

    lax.fori_loop(0, out.shape[0] // 256, finish, 0)


def node_kernel(here, feats, cot, t0, t1, t2, t3, other, base, down_t, up, new_out, keep, give, partial_out, grads):
    first = here[0] == 0
    full = feats.shape[1]
    half = full // 2
    nodes = feats.shape[0]
    mine = add(t0[:nodes], t1[:nodes], t2[:nodes], t3[...]).astype(BF)
    rest = other[...]
    agg = [jnp.where(first, mine, rest), jnp.where(first, rest, mine)]
    joined = jnp.concatenate([feats[...]] + agg, axis=1)
    low = times_transposed(joined, down_t[...]).astype(BF)
    pre = dot(joined, base[...]) + dot(low, up[...])
    sigma = sigmoid(pre)
    cot_wide = cot[...].astype(F32)
    slope = (cot_wide * (sigma * (1.0 + pre * (1.0 - sigma)))).astype(BF)
    mix = times_transposed(slope, up[...]).astype(BF)
    joined_grad = times_transposed(slope, base[...]) + dot(mix, down_t[...])
    agg_grad = joined_grad[:, full:].astype(BF)
    width = half // 2
    left = here[2] == 0
    for out, values in (
        (keep, jnp.where(first, agg_grad[:, :half], agg_grad[:, half:])),
        (give, jnp.where(first, agg_grad[:, half:], agg_grad[:, :half])),
    ):
        out[:nodes] = jnp.where(left, values[:, :width], values[:, width:])
        out[nodes:] = jnp.where(left, values[:, width:], values[:, :width])
    new_out[...] = (feats[...].astype(F32) + pre * sigma).astype(BF)
    partial_out[...] = cot_wide + joined_grad[:, :full]
    grads[:, : 2 * full] = across(mix, joined)
    grads[:, 2 * full :] = across(low, slope)


def edge_kernel(feats, parts, partial, base, down_t, up, feat_out, grads):
    full = feats.shape[1]
    low = times_transposed(feats[...], down_t[...]).astype(BF)
    pre = dot(feats[...], base[...]) + dot(low, up[...])
    factor = silu_slope(pre)
    quarters = [None] * 4
    for i in range(parts.shape[0]):
        term = parts[i].astype(F32)
        quarters[i % 4] = term if quarters[i % 4] is None else quarters[i % 4] + term
    slope = (jnp.concatenate(quarters, axis=1) * factor).astype(BF)
    mix = times_transposed(slope, up[...]).astype(BF)
    grads[:, :full] = across(mix, feats[...])
    grads[:, full:] = across(low, slope)
    feat_out[...] = (
        partial[...] + times_transposed(slope, base[...]) + dot(mix, down_t[...])
    ).astype(BF)


def exchange(pieces, axes):
    shape = pieces.shape
    flat = pieces.reshape(shape[0] * shape[1], shape[2])
    return lax.all_to_all(flat, axes, split_axis=0, concat_axis=0, tiled=True)


def sum_over_all(grads):
    n_near, n_z = lax.axis_size(NEAR), lax.axis_size("z")
    rank, wide = grads.shape
    lines = -(-rank * wide // (n_near * 2048)) * 16
    grads = jnp.pad(grads.astype(BF).reshape(-1), (0, n_near * lines * 128 - rank * wide))
    mine = exchange(grads.reshape(n_near, lines, 128), NEAR)
    mine = mine.reshape(n_near, lines, 128).astype(F32).sum(axis=0).astype(BF)
    spread = jnp.broadcast_to(mine[None], (n_z, lines, 128))
    mine = exchange(spread, "z").reshape(n_z, lines, 128).astype(F32).sum(axis=0).astype(BF)
    spread = jnp.broadcast_to(mine[None], (n_near, lines, 128))
    whole = exchange(spread, NEAR).astype(F32).reshape(-1)
    return whole[: rank * wide].reshape(rank, wide)


def body(
    node_feats,
    cotangent,
    edge_base,
    edge_down,
    edge_up,
    node_base,
    node_down,
    node_up,
    tile_weight,
    tile_place,
    tile_count,
):
    nodes, full = node_feats.shape
    n_row = lax.axis_size(ROW)
    n_col = lax.axis_size(COL)
    n_z = lax.axis_size("z")
    n_up, n_down = n_z // 2, (n_z - 1) // 2
    rank = edge_up.shape[0]
    half, width = full // 2, full // 4
    tiles = tile_weight[0, 0]
    slots = tiles.shape[0]
    sds = jax.ShapeDtypeStruct

    def swap(values, axis):
        return lax.ppermute(values, axis, [(0, 1), (1, 0)])

    def up(values):
        return lax.ppermute(values, "z", [(i, (i + 1) % n_z) for i in range(n_z)])

    def down(values):
        return lax.ppermute(values, "z", [((i + 1) % n_z, i) for i in range(n_z)])

    meta = jnp.concatenate([tile_place.reshape(1, 2 * slots), tile_count.reshape(1, 1)], axis=1)
    meta = jnp.pad(meta, ((0, 0), (0, 256 - meta.shape[1])))
    meta = jnp.concatenate([meta, swap(meta, "co")], axis=0)
    tiles_c = swap(tiles, "co")
    meta = jnp.concatenate([meta, swap(meta, "xh")], axis=0)
    here = jnp.stack([lax.axis_index("co"), lax.axis_index("z"), lax.axis_index("xh")])
    here = here.astype(jnp.int32)

    pieces = call(
        message_kernel,
        (sds((n_row, nodes, half), BF),),
        node_feats,
        edge_base,
        edge_down.T,
        edge_up,
        name="message",
    )[0]
    source = exchange(pieces, ROW)

    flat = [d for i in range(n_up) for d in (n_up - i, i - n_down)]
    mirror = {d: d if d == n_up else -d for d in flat}
    first, second = flat[: n_z // 2], flat[n_z // 2 :]
    groups = [[(1, mirror[d], 1) for d in part] for part in (first, second)]
    groups += [[(0, d, 0), (0, d, 1)] for d in flat] + [[(1, mirror[d], 0)] for d in flat]

    def forward(*refs):
        forward_kernel(groups, n_z, *refs)

    outs = call(
        forward,
        tuple(sds((len(places) * nodes, half), BF) for places in groups),
        here,
        meta,
        tiles,
        tiles_c,
        source,
        scratch=[
            pltpu.VMEM((2 * n_col * nodes + 128, half), F32),
            pltpu.VMEM((2, slots, 128, 128), BF),
            pltpu.SemaphoreType.DMA((2 * PARTS,)),
        ],
        smem=2,
        far=(2, 3),
        flops=4 * slots * 128 * 128 * half,
        name="tiles",
    )
    sent, own, kept = outs[:2], dict(zip(flat, outs[2 : 2 + n_z])), outs[2 + n_z :]
    got = [swap(block, "xh") for block in sent]
    tiles_near, got[0] = lax.optimization_barrier((tiles[: slots // 2], got[0]))
    tiles_x = [swap(tiles_near, "xh")]
    other = {}
    for i, d in enumerate(flat):
        k = i % len(first)
        other[d] = add(kept[i], got[i // len(first)][k * nodes : (k + 1) * nodes]).astype(BF)

    def ring_sum(blocks, up, down):
        rising = up(blocks[n_up])
        falling = down(blocks[-n_down]) if n_down else jnp.zeros_like(rising)
        for k in range(1, n_up):
            rising = up(add(rising, blocks[n_up - k]).astype(BF))
            if k < n_down:
                falling = down(add(falling, blocks[k - n_down]).astype(BF))
        return [blocks[0], rising, falling]

    terms = ring_sum(own, up, down)
    agg_other = add(*ring_sum(other, down, up)).astype(BF)
    agg_other, tiles_x[0] = lax.optimization_barrier((agg_other, tiles_x[0]))
    agg_other = swap(agg_other, "co")
    across_x = swap(add(*[term[nodes:] for term in terms]).astype(BF), "xh")
    new_feats, keep, give, partial_grad, node_grads = call(
        node_kernel,
        (
            sds((nodes, full), BF),
            sds((2 * nodes, width), BF),
            sds((2 * nodes, width), BF),
            sds((nodes, full), F32),
            sds((rank, 3 * full), F32),
        ),
        here,
        node_feats,
        cotangent,
        *terms,
        across_x,
        agg_other,
        node_base,
        node_down.T,
        node_up,
        smem=1,
        name="node",
    )

    tiles_cx = [swap(lax.optimization_barrier((tiles_x[0], keep))[0], "co")]
    both = jnp.stack([keep, swap(give, "co")]).reshape(2, 2, nodes, width)
    beyond = swap(both[:, 1].reshape(2 * nodes, width), "xh")
    tiles_near, beyond = lax.optimization_barrier((tiles[slots // 2 :], beyond))
    tiles_x.append(swap(tiles_near, "xh"))
    beyond = beyond.reshape(2, nodes, width)
    shards = {0: jnp.stack([both[:, 0], beyond], axis=1).reshape(4 * nodes, width)}
    for k in range(1, n_up + 1):
        shards[-k] = up(shards[1 - k])
        if k <= n_down:
            shards[k] = down(shards[k - 1])

    late = [1 - n_up, n_down] if n_down else [0]
    tiles_x[1] = lax.optimization_barrier([tiles_x[1]] + [shards[d] for d in late])[0]
    tiles_cx.append(swap(tiles_x[1], "co"))

    def backward(*refs):
        backward_kernel(list(shards), n_z, *refs)

    rows = 2 * n_row * nodes
    partial_cols = call(
        backward,
        (sds((rows, width), BF),),
        here,
        meta,
        tiles,
        tiles_c,
        *tiles_x,
        *tiles_cx,
        *shards.values(),
        scratch=[
            pltpu.VMEM((rows + 128, width), F32),
            pltpu.VMEM((2 * n_col * nodes, width), BF),
            pltpu.VMEM((4, slots, 128, 128), BF),
            pltpu.SemaphoreType.DMA((4 * PARTS,)),
        ],
        smem=2,
        far=(2, 3, 4, 5, 6, 7),
        flops=8 * slots * 128 * 128 * width,
        name="tiles_back",
    )[0]
    parts = exchange(partial_cols.reshape(2 * n_row, nodes, width), NEAR)
    feat_grad, edge_grads = call(
        edge_kernel,
        (sds((nodes, full), BF), sds((rank, 2 * full), F32)),
        node_feats,
        parts.reshape(2 * n_row, nodes, width),
        partial_grad,
        edge_base,
        edge_down.T,
        edge_up,
        name="edge",
    )
    grads = sum_over_all(jnp.concatenate([edge_grads, node_grads], axis=1))
    grads = grads * (1.0 / math.sqrt(nodes * n_row * n_col))
    return (
        new_feats,
        feat_grad,
        grads[:, :full].T,
        grads[:, full : 2 * full],
        grads[:, 2 * full : 4 * full].T,
        grads[:, 4 * full :],
    )


def solution(mesh):
    n_row, n_col = mesh.shape["row"], mesh.shape["col"]
    fine = Mesh(mesh.devices.reshape(n_row // 2, 2, n_col // 2, 2), ALL)
    nodes = P(ROW + COL, None)
    placed = (
        nodes,
        nodes,
        P(),
        P(),
        P(),
        P(),
        P(),
        P(),
        P(ROW, COL, None, None, None),
        P(ROW, COL, None, None),
        P(ROW, COL),
    )
    return jax.shard_map(
        body,
        mesh=fine,
        in_specs=placed,
        out_specs=(nodes, nodes, P(), P(), P(), P()),
        check_vma=False,
    )
```

```python
import math

import jax
import jax.numpy as jnp
from jax import lax
from jax.experimental import pallas as pl
from jax.experimental.pallas import tpu as pltpu
from jax.sharding import Mesh, PartitionSpec as P

BF, F32 = jnp.bfloat16, jnp.float32
UNROLL = 16
PARTS = 2
MIB = 1 << 20
ALL = ("xly", "co", "z", "xh")
ROW, COL = ("xly", "co"), ("z", "xh")
NEAR = ("xly", "co", "xh")
SHARED = ((0, 0), (1, 0), (0, 1), (1, 1))


def dot(left, right):
    return jnp.dot(left, right, preferred_element_type=F32)


def across(left, right):
    return lax.dot_general(left, right, (((0,), (0,)), ((), ())), preferred_element_type=F32)


def times_transposed(left, right):
    return lax.dot_general(left, right, (((1,), (1,)), ((), ())), preferred_element_type=F32)


def sigmoid(values):
    return 1.0 / (1.0 + jnp.exp(-values))


def silu_slope(values):
    sigma = sigmoid(values)
    return sigma * (1.0 + values * (1.0 - sigma))


def call(kernel, out_shape, *args, scratch=(), smem=0, vmem=40, flops=0, name=None, far=()):
    def place(i):
        return pl.BlockSpec(memory_space=pltpu.HBM if i in far else pltpu.VMEM)

    moved = sum(a.size * a.dtype.itemsize for a in args)
    moved += sum(math.prod(s.shape) * s.dtype.itemsize for s in jax.tree.leaves(out_shape))
    return pl.pallas_call(
        kernel,
        out_shape=out_shape,
        in_specs=[pl.BlockSpec(memory_space=pltpu.SMEM)] * smem
        + [place(i) for i in range(smem, len(args))],
        out_specs=(pl.BlockSpec(memory_space=pltpu.VMEM),) * len(out_shape),
        scratch_shapes=list(scratch),
        compiler_params=pltpu.CompilerParams(vmem_limit_bytes=vmem * MIB),
        cost_estimate=pl.CostEstimate(flops=flops, bytes_accessed=moved, transcendentals=0),
        name=name,
    )(*args)


def add(*terms):
    total = terms[0].astype(F32)
    for term in terms[1:]:
        total = total + term.astype(F32)
    return total


def message_kernel(feats, base, down_t, up, pieces):
    low = times_transposed(feats[...], down_t[...]).astype(BF)
    pre = dot(feats[...], base[...]) + dot(low, up[...])
    message = (pre * sigmoid(pre)).astype(BF)
    width = pieces.shape[2]
    for i in range(pieces.shape[0]):
        pieces[i] = message[:, i % 2 * width : (i % 2 + 1) * width]


def clear(total):
    rows = total.shape[0] - 128

    def step(i, carry):
        at = pl.ds(pl.multiple_of(i * 256, 256), 256)
        total[at, :] = jnp.zeros((256, total.shape[1]), F32)
        return carry

    lax.fori_loop(0, rows // 256, step, 0)


def fetch_tiles(meta, stacks, near, sems):
    slots = near.shape[1]
    size = slots // PARTS
    copies = []
    for owner, stack in enumerate(stacks):
        for part in range(PARTS):
            at = pl.ds(part * size, size)
            source = stack[0].at[at] if len(stack) == 1 else stack[part]
            live = meta[owner, 2 * slots] > part * size
            copy = pltpu.make_async_copy(
                source, near.at[owner, at], sems.at[owner * PARTS + part]
            )
            pl.when(live)(copy.start)
            copies.append((live, copy))
    return copies


def add_tiles(meta, owner, weights, copies, source, total, row_at, col_at, backward):
    slots = weights.shape[0]
    spare = total.shape[0] - 128
    count = meta[owner, 2 * slots]
    size = slots // PARTS

    def group(i, carry):
        products, places = [], []
        for j in range(UNROLL):
            slot = i * UNROLL + j
            live = slot < count
            row = row_at(jnp.where(live, meta[owner, 2 * slot], 0))
            col = col_at(jnp.where(live, meta[owner, 2 * slot + 1], 0))
            begin, end = (row, col) if backward else (col, row)
            places.append(pl.multiple_of(jnp.where(live, end, spare), 128))
            block = source[pl.ds(pl.multiple_of(begin, 128), 128), :]
            tile = weights[slot]
            products.append(across(tile, block) if backward else dot(tile, block))
        for product, at in zip(products, places):
            total[pl.ds(at, 128), :] += product
        return carry

    for part, (wanted, copy) in enumerate(copies):
        pl.when(wanted)(copy.wait)
        end = jnp.minimum(count, (part + 1) * size)
        lax.fori_loop(part * size // UNROLL, (end + UNROLL - 1) // UNROLL, group, 0)


def forward_kernel(groups, n_z, here, meta, w0, w1, source, *rest):
    outs, (total, near, sems) = rest[:-3], rest[-3:]
    copies = fetch_tiles(meta, [[w0], [w1]], near, sems)
    z, xh = here[1], here[2]
    nodes = (total.shape[0] - 128) // (4 * n_z)
    clear(total)
    for owner in range(2):

        def row_at(tile, owner=owner):
            return owner * (2 * n_z * nodes) + tile * 128

        def col_at(tile):
            return tile * 128

        parts = copies[owner * PARTS : (owner + 1) * PARTS]
        add_tiles(meta, owner, near.at[owner], parts, source, total, row_at, col_at, False)
    for out, places in zip(outs, groups):
        for k, (owner, distance, side) in enumerate(places):
            to = lax.rem(z + (distance + n_z), n_z) * 2 + (xh ^ side)
            at = pl.multiple_of((owner * 2 * n_z + to) * nodes, nodes)
            out[k * nodes : (k + 1) * nodes] = total[pl.ds(at, nodes), :].astype(BF)


def backward_kernel(distances, n_z, here, meta, w0, w1, w2, w3, w4, w5, *rest):
    shards, (out, total, source, near, sems) = rest[:-5], rest[-5:]
    copies = fetch_tiles(meta, [[w0], [w1], [w2, w3], [w4, w5]], near, sems)
    z, xh = here[1], here[2]
    block = source.shape[0] // n_z
    nodes = block // 4
    for shard, distance in zip(shards, distances):
        at = lax.rem(z + (distance + n_z), n_z) * block
        source[pl.ds(pl.multiple_of(at, block), block), :] = shard[...]
    clear(total)
    for owner, (core, side) in enumerate(SHARED):

        def row_at(tile, core=core):
            place = core * 2 + (((tile >> 1) & 1) ^ xh)
            return (tile >> 2) * block + place * nodes + (tile & 1) * 128

        def col_at(tile, side=side):
            return ((tile >> 1) * 2 + (xh ^ side)) * nodes + (tile & 1) * 128

        parts = copies[owner * PARTS : (owner + 1) * PARTS]
        add_tiles(meta, owner, near.at[owner], parts, source, total, row_at, col_at, True)

    def finish(i, carry):
        at = pl.ds(pl.multiple_of(i * 256, 256), 256)
        out[at, :] = total[at, :].astype(BF)
        return carry

    lax.fori_loop(0, out.shape[0] // 256, finish, 0)


def node_kernel(here, feats, cot, t0, t1, t2, t3, other, base, down_t, up, new_out, keep, give, partial_out, grads):
    first = here[0] == 0
    full = feats.shape[1]
    half = full // 2
    nodes = feats.shape[0]
    mine = add(t0[:nodes], t1[:nodes], t2[:nodes], t3[...]).astype(BF)
    rest = other[...]
    agg = [jnp.where(first, mine, rest), jnp.where(first, rest, mine)]
    joined = jnp.concatenate([feats[...]] + agg, axis=1)
    low = times_transposed(joined, down_t[...]).astype(BF)
    pre = dot(joined, base[...]) + dot(low, up[...])
    sigma = sigmoid(pre)
    cot_wide = cot[...].astype(F32)
    slope = (cot_wide * (sigma * (1.0 + pre * (1.0 - sigma)))).astype(BF)
    mix = times_transposed(slope, up[...]).astype(BF)
    joined_grad = times_transposed(slope, base[...]) + dot(mix, down_t[...])
    agg_grad = joined_grad[:, full:].astype(BF)
    width = half // 2
    left = here[2] == 0
    for out, values in (
        (keep, jnp.where(first, agg_grad[:, :half], agg_grad[:, half:])),
        (give, jnp.where(first, agg_grad[:, half:], agg_grad[:, :half])),
    ):
        out[:nodes] = jnp.where(left, values[:, :width], values[:, width:])
        out[nodes:] = jnp.where(left, values[:, width:], values[:, :width])
    new_out[...] = (feats[...].astype(F32) + pre * sigma).astype(BF)
    partial_out[...] = cot_wide + joined_grad[:, :full]
    grads[:, : 2 * full] = across(mix, joined)
    grads[:, 2 * full :] = across(low, slope)


def edge_kernel(feats, parts, partial, base, down_t, up, feat_out, grads):
    full = feats.shape[1]
    low = times_transposed(feats[...], down_t[...]).astype(BF)
    pre = dot(feats[...], base[...]) + dot(low, up[...])
    factor = silu_slope(pre)
    quarters = [None] * 4
    for i in range(parts.shape[0]):
        term = parts[i].astype(F32)
        quarters[i % 4] = term if quarters[i % 4] is None else quarters[i % 4] + term
    slope = (jnp.concatenate(quarters, axis=1) * factor).astype(BF)
    mix = times_transposed(slope, up[...]).astype(BF)
    grads[:, :full] = across(mix, feats[...])
    grads[:, full:] = across(low, slope)
    feat_out[...] = (
        partial[...] + times_transposed(slope, base[...]) + dot(mix, down_t[...])
    ).astype(BF)


def exchange(pieces, axes):
    shape = pieces.shape
    flat = pieces.reshape(shape[0] * shape[1], shape[2])
    return lax.all_to_all(flat, axes, split_axis=0, concat_axis=0, tiled=True)


def sum_over_all(grads):
    n_near, n_z = lax.axis_size(NEAR), lax.axis_size("z")
    rank, wide = grads.shape
    lines = -(-rank * wide // (n_near * 2048)) * 16
    grads = jnp.pad(grads.astype(BF).reshape(-1), (0, n_near * lines * 128 - rank * wide))
    mine = exchange(grads.reshape(n_near, lines, 128), NEAR)
    mine = mine.reshape(n_near, lines, 128).astype(F32).sum(axis=0).astype(BF)
    spread = jnp.broadcast_to(mine[None], (n_z, lines, 128))
    mine = exchange(spread, "z").reshape(n_z, lines, 128).astype(F32).sum(axis=0).astype(BF)
    spread = jnp.broadcast_to(mine[None], (n_near, lines, 128))
    whole = exchange(spread, NEAR).astype(F32).reshape(-1)
    return whole[: rank * wide].reshape(rank, wide)


def body(
    node_feats,
    cotangent,
    edge_base,
    edge_down,
    edge_up,
    node_base,
    node_down,
    node_up,
    tile_weight,
    tile_place,
    tile_count,
):
    nodes, full = node_feats.shape
    n_row = lax.axis_size(ROW)
    n_col = lax.axis_size(COL)
    n_z = lax.axis_size("z")
    n_up, n_down = n_z // 2, (n_z - 1) // 2
    rank = edge_up.shape[0]
    half, width = full // 2, full // 4
    tiles = tile_weight[0, 0]
    slots = tiles.shape[0]
    sds = jax.ShapeDtypeStruct

    def swap(values, axis):
        return lax.ppermute(values, axis, [(0, 1), (1, 0)])

    def up(values):
        return lax.ppermute(values, "z", [(i, (i + 1) % n_z) for i in range(n_z)])

    def down(values):
        return lax.ppermute(values, "z", [((i + 1) % n_z, i) for i in range(n_z)])

    meta = jnp.concatenate([tile_place.reshape(1, 2 * slots), tile_count.reshape(1, 1)], axis=1)
    meta = jnp.pad(meta, ((0, 0), (0, 256 - meta.shape[1])))
    meta = jnp.concatenate([meta, swap(meta, "co")], axis=0)
    tiles_c = swap(tiles, "co")
    meta = jnp.concatenate([meta, swap(meta, "xh")], axis=0)
    here = jnp.stack([lax.axis_index("co"), lax.axis_index("z"), lax.axis_index("xh")])
    here = here.astype(jnp.int32)

    pieces = call(
        message_kernel,
        (sds((n_row, nodes, half), BF),),
        node_feats,
        edge_base,
        edge_down.T,
        edge_up,
        name="message",
    )[0]
    source = exchange(pieces, ROW)

    flat = [d for i in range(n_up) for d in (n_up - i, i - n_down)]
    mirror = {d: d if d == n_up else -d for d in flat}
    first, second = flat[: n_z // 2], flat[n_z // 2 :]
    groups = [[(1, mirror[d], 1) for d in part] for part in (first, second)]
    groups += [[(0, d, 0), (0, d, 1)] for d in flat] + [[(1, mirror[d], 0)] for d in flat]

    def forward(*refs):
        forward_kernel(groups, n_z, *refs)

    outs = call(
        forward,
        tuple(sds((len(places) * nodes, half), BF) for places in groups),
        here,
        meta,
        tiles,
        tiles_c,
        source,
        scratch=[
            pltpu.VMEM((2 * n_col * nodes + 128, half), F32),
            pltpu.VMEM((2, slots, 128, 128), BF),
            pltpu.SemaphoreType.DMA((2 * PARTS,)),
        ],
        smem=2,
        far=(2, 3),
        flops=4 * slots * 128 * 128 * half,
        name="tiles",
    )
    sent, own, kept = outs[:2], dict(zip(flat, outs[2 : 2 + n_z])), outs[2 + n_z :]
    got = [swap(block, "xh") for block in sent]
    tiles_near, got[0] = lax.optimization_barrier((tiles[: slots // 2], got[0]))
    tiles_x = [swap(tiles_near, "xh")]
    other = {}
    for i, d in enumerate(flat):
        k = i % len(first)
        other[d] = add(kept[i], got[i // len(first)][k * nodes : (k + 1) * nodes]).astype(BF)

    def ring_sum(blocks, up, down):
        rising = up(blocks[n_up])
        falling = down(blocks[-n_down]) if n_down else jnp.zeros_like(rising)
        for k in range(1, n_up):
            rising = up(add(rising, blocks[n_up - k]).astype(BF))
            if k < n_down:
                falling = down(add(falling, blocks[k - n_down]).astype(BF))
        return [blocks[0], rising, falling]

    terms = ring_sum(own, up, down)
    agg_other = add(*ring_sum(other, down, up)).astype(BF)
    agg_other, tiles_x[0] = lax.optimization_barrier((agg_other, tiles_x[0]))
    agg_other = swap(agg_other, "co")
    across_x = swap(add(*[term[nodes:] for term in terms]).astype(BF), "xh")
    new_feats, keep, give, partial_grad, node_grads = call(
        node_kernel,
        (
            sds((nodes, full), BF),
            sds((2 * nodes, width), BF),
            sds((2 * nodes, width), BF),
            sds((nodes, full), F32),
            sds((rank, 3 * full), F32),
        ),
        here,
        node_feats,
        cotangent,
        *terms,
        across_x,
        agg_other,
        node_base,
        node_down.T,
        node_up,
        smem=1,
        name="node",
    )

    tiles_cx = [swap(lax.optimization_barrier((tiles_x[0], keep))[0], "co")]
    both = jnp.stack([keep, swap(give, "co")]).reshape(2, 2, nodes, width)
    beyond = swap(both[:, 1].reshape(2 * nodes, width), "xh")
    tiles_near, beyond = lax.optimization_barrier((tiles[slots // 2 :], beyond))
    tiles_x.append(swap(tiles_near, "xh"))
    beyond = beyond.reshape(2, nodes, width)
    shards = {0: jnp.stack([both[:, 0], beyond], axis=1).reshape(4 * nodes, width)}
    for k in range(1, n_up + 1):
        shards[-k] = up(shards[1 - k])
        if k <= n_down:
            shards[k] = down(shards[k - 1])

    late = [-n_up, n_down] if n_down else [0]
    tiles_x[1] = lax.optimization_barrier([tiles_x[1]] + [shards[d] for d in late])[0]
    tiles_cx.append(swap(tiles_x[1], "co"))

    def backward(*refs):
        backward_kernel(list(shards), n_z, *refs)

    rows = 2 * n_row * nodes
    partial_cols = call(
        backward,
        (sds((rows, width), BF),),
        here,
        meta,
        tiles,
        tiles_c,
        *tiles_x,
        *tiles_cx,
        *shards.values(),
        scratch=[
            pltpu.VMEM((rows + 128, width), F32),
            pltpu.VMEM((2 * n_col * nodes, width), BF),
            pltpu.VMEM((4, slots, 128, 128), BF),
            pltpu.SemaphoreType.DMA((4 * PARTS,)),
        ],
        smem=2,
        far=(2, 3, 4, 5, 6, 7),
        flops=8 * slots * 128 * 128 * width,
        name="tiles_back",
    )[0]
    parts = exchange(partial_cols.reshape(2 * n_row, nodes, width), NEAR)
    feat_grad, edge_grads = call(
        edge_kernel,
        (sds((nodes, full), BF), sds((rank, 2 * full), F32)),
        node_feats,
        parts.reshape(2 * n_row, nodes, width),
        partial_grad,
        edge_base,
        edge_down.T,
        edge_up,
        name="edge",
    )
    grads = sum_over_all(jnp.concatenate([edge_grads, node_grads], axis=1))
    grads = grads * (1.0 / math.sqrt(nodes * n_row * n_col))
    return (
        new_feats,
        feat_grad,
        grads[:, :full].T,
        grads[:, full : 2 * full],
        grads[:, 2 * full : 4 * full].T,
        grads[:, 4 * full :],
    )


def solution(mesh):
    n_row, n_col = mesh.shape["row"], mesh.shape["col"]
    fine = Mesh(mesh.devices.reshape(n_row // 2, 2, n_col // 2, 2), ALL)
    nodes = P(ROW + COL, None)
    placed = (
        nodes,
        nodes,
        P(),
        P(),
        P(),
        P(),
        P(),
        P(),
        P(ROW, COL, None, None, None),
        P(ROW, COL, None, None),
        P(ROW, COL),
    )
    return jax.shard_map(
        body,
        mesh=fine,
        in_specs=placed,
        out_specs=(nodes, nodes, P(), P(), P(), P()),
        check_vma=False,
    )
```
